256 devices in a mesh: dp: 64 (over z, y, core), rep: 4 (over x).
Axes of the slice: x: 4, y: 4, z: 8, core: 2. Of those that a mesh axis runs over, the one named last changes fastest.
Arguments:
- grads: bfloat16 [256, 4096, 512], P(('dp', 'rep')), may hold values from -1000 to 1000
- master: float32 [4096, 512], P('dp'), may hold values from -3 to 3
- first_moment: float32 [4096, 512], P('dp'), may hold values from -2 to 2
- second_moment: float32 [4096, 512], P('dp'), may hold values from 0.01 to 1
Outputs:
- weights: bfloat16 [4096, 512], replicated
- new_master: float32 [4096, 512], P('dp')
- new_first: float32 [4096, 512], P('dp')
- new_second: float32 [4096, 512], P('dp')
The draws below stay inside these ranges and needn't reach their ends.
All inputs are finite; a program needn't handle non-finite values.
Results may differ from the reference program's by a relative error of at most 0.001.
Values may be sent and summed in bfloat16 or wider, within the bound.
No kernel may reach another device: no remote copies, remote signals or barrier semaphores. Data moves between devices by JAX's collectives and lax.ppermute only.
A program may use at most 64 MiB of HBM per device.

```python
import math
import jax
import jax.numpy as jnp
from jax import lax

D_WIN = 4096
STEP = 20
COLS = 512
SOURCES = 256
N_REP = 4


def draw_grads(key, part):
    keys = jax.random.split(jax.random.fold_in(key, 11), 3)
    position = jnp.arange(D_WIN, dtype=jnp.float32) / D_WIN
    replica = (jnp.arange(SOURCES, dtype=jnp.int32) % N_REP).astype(jnp.float32) / max(N_REP - 1, 1)
    row_scale = 10.0 ** jax.random.uniform(keys[0], (D_WIN,), jnp.float32) * 5.0 ** position
    col_scale = 10.0 ** jax.random.uniform(keys[1], (COLS,), jnp.float32)
    base = jax.random.normal(keys[2], (SOURCES, D_WIN, COLS), jnp.float32)
    base = base * (1.0 + 2.0 * replica)[:, None, None]
    scaled = base * row_scale[None, :, None] * col_scale[None, None, :]
    return jnp.clip(scaled, -1000.0, 1000.0).astype(jnp.bfloat16)


def block_levels(rng, shape, cuts, low, largest):
    level, own = 1.0, jax.random.fold_in(rng, 6)
    for axis_at, blocks in cuts:
        steps = jnp.exp(jax.random.uniform(jax.random.fold_in(own, axis_at), (blocks,), jnp.float32, low / len(cuts), largest / len(cuts)))
        level = level * jnp.repeat(steps, shape[axis_at] // blocks).reshape([-1 if axis == axis_at else 1 for axis in range(len(shape))])
    return level


def scatter_about(rng, dims, width, limit, cuts=(), held_as=jnp.bfloat16):
    values = width * jax.random.normal(rng, dims, jnp.float32)
    if cuts:
        values = values * block_levels(rng, dims, cuts, -0.22, 0.18)
    return jnp.clip(values, -limit, limit).astype(held_as)


def setup_inputs(seed: int = 0) -> dict:
    splits = jax.random.split(jax.random.key(seed), 5)
    return {
        "grads": draw_grads(jax.random.fold_in(splits[4], 71), 0),
        "master": scatter_about(splits[1], (D_WIN, COLS), 0.5, 3.0, ((0, 64),), jnp.float32),
        "first_moment": scatter_about(splits[2], (D_WIN, COLS), 0.3, 2.0, ((0, 64),), jnp.float32),
        "second_moment": jnp.clip(jnp.exp(math.log(1.0) - 4.6051702 * jax.random.uniform(splits[3], (D_WIN, COLS), jnp.float32) ** block_levels(splits[3], (D_WIN, COLS), ((0, 64),), -0.2, 0.2)), 0.01, 1.0),
    }


def adam_update(clipped, master, first_moment, second_moment):
    new_first = 0.9 * first_moment + 0.1 * clipped
    new_second = 0.95 * second_moment + 0.05 * clipped * clipped
    first_hat = new_first / (1.0 - 0.9 ** STEP)
    second_hat = new_second / (1.0 - 0.95 ** STEP)
    update = first_hat / (jnp.sqrt(second_hat) + 1e-08)
    new_master = master - 0.01 * (update + 0.1 * master)
    return (new_master, new_first, new_second)

def reference(grads, master, first_moment, second_moment):

    def accumulate(index, total):
        piece = lax.dynamic_index_in_dim(grads, index, 0, keepdims=False)
        return total + piece.astype(jnp.float32)
    total = lax.fori_loop(0, SOURCES, accumulate, jnp.zeros((D_WIN, COLS), jnp.float32))
    norm = jnp.sqrt(jnp.sum(total * total))
    threshold = 4.0 * math.sqrt(D_WIN * COLS)
    factor = jnp.minimum(1.0, threshold / (norm + 1e-06))
    new_master, new_first, new_second = adam_update(factor * total, master, first_moment, second_moment)
    return (new_master.astype(jnp.bfloat16), new_master, new_first, new_second)
```

```python
import math

import jax
import jax.numpy as jnp
from jax import lax
from jax.sharding import Mesh
from jax.sharding import PartitionSpec as P

D_WIN = 4096
STEP = 20
AXES = ("zh", "zl", "y", "c", "x")
GROUP = ("zl", "y", "c", "x")


def to_all(block, axes):
    length = lax.axis_size(axes)
    return lax.all_to_all(
        jnp.broadcast_to(block[None], (length, *block.shape)), axes, 0, 0, tiled=True
    )


def adam_update(clipped, master, first_moment, second_moment):
    new_first = 0.9 * first_moment + 0.1 * clipped
    new_second = 0.95 * second_moment + 0.05 * clipped * clipped
    first_hat = new_first / (1.0 - 0.9**STEP)
    second_hat = new_second / (1.0 - 0.95**STEP)
    update = first_hat / (jnp.sqrt(second_hat) + 1e-08)
    new_master = master - 0.01 * (update + 0.1 * master)
    return (new_master, new_first, new_second)


def clip_factor(squares, width):
    threshold = 4.0 * math.sqrt(D_WIN * width)
    return jnp.minimum(1.0, threshold / (jnp.sqrt(squares) + 1e-06))


def ring(block, axis):
    n = lax.axis_size(axis)
    return [
        lax.ppermute(block, axis, [(i, (i + k) % n) for i in range(n)]) for k in range(1, n)
    ]


def gather_ring(block, axis):
    n = lax.axis_size(axis)
    me = lax.axis_index(axis)
    parts = [block] + ring(block, axis)
    out = jnp.zeros((n, *block.shape), block.dtype)
    for k, part in enumerate(parts):
        out = lax.dynamic_update_index_in_dim(out, part, lax.rem(me - k + n, n), 0)
    return out


def body(grads, master, first_moment, second_moment):
    width = grads.shape[2]
    zh, zl, y, c, x = (lax.axis_size(a) for a in AXES)
    rows = master.shape[0] // x
    me_x = lax.axis_index("x")
    me_zh = lax.axis_index("zh")

    own = jnp.concatenate([
        lax.dynamic_slice_in_dim(a, me_x * rows, rows, 0)
        for a in (master, first_moment, second_moment)
    ])
    states = gather_ring(own, "zh")
    states = states.reshape(zh, 3, rows, width).transpose(1, 0, 2, 3).reshape(3, zh * rows, width)

    local = grads[0].reshape(zh, zl, y, c, x, rows, width)
    local = local.transpose(1, 2, 3, 4, 0, 5, 6).reshape(-1, zh * rows, width)
    pieces = lax.all_to_all(local, GROUP, 0, 0, tiled=True)
    partial = jnp.sum(pieces.astype(jnp.float32), axis=0)
    total = jnp.sum(to_all(partial, "zh"), axis=0)

    mine = lax.dynamic_slice_in_dim(total, me_zh * rows, rows, 0)
    owned = gather_ring(mine, "x").reshape(-1, width)

    squares = jnp.sum(to_all(jnp.sum(total * total), GROUP))
    factor = clip_factor(squares, width)

    ahead = adam_update(factor * total, states[0], states[1], states[2])[0]
    gathered = to_all(ahead.astype(jnp.bfloat16), ("zl", "y", "x"))
    both = to_all(gathered, "c")
    weights = both.reshape(c, zl, y, x, zh, rows, width).transpose(4, 1, 2, 0, 3, 5, 6)
    weights = weights.reshape(-1, width)

    new_master, new_first, new_second = adam_update(
        factor * owned, master, first_moment, second_moment
    )
    return (weights, new_master, new_first, new_second)


def solution(mesh):
    split = Mesh(mesh.devices.reshape(4, 2, 4, 2, mesh.shape["rep"]), AXES)
    dp = AXES[:4]
    placed = (P(AXES, None, None), P(dp, None), P(dp, None), P(dp, None))
    return jax.shard_map(
        body,
        mesh=split,
        in_specs=placed,
        out_specs=(P(), P(dp, None), P(dp, None), P(dp, None)),
        check_vma=False,
    )
```

```python
import math

import jax
import jax.numpy as jnp
from jax import lax
from jax.sharding import Mesh
from jax.sharding import PartitionSpec as P

D_WIN = 4096
STEP = 20
AXES = ("zh", "zl", "y", "c", "x")
PLANE = ("zl", "y", "x")
OWNERS = ("zl", "y", "c", "x")
SWAP = [(0, 1), (1, 0)]


def to_all(block, axes):
    length = lax.axis_size(axes)
    return lax.all_to_all(
        jnp.broadcast_to(block[None], (length, *block.shape)), axes, 0, 0, tiled=True
    )


def neighbour(block, axis, mask):
    return lax.ppermute(block, axis, [(i, i ^ mask) for i in range(4)])


def sum_of_four(block, axis):
    for mask in (1, 3):
        block = block + neighbour(block, axis, mask)
    return block


def gather_of_four(block, axis):
    me = lax.axis_index(axis)
    block = block[None]
    for mask, low in ((1, me % 2 == 0), (3, me < 2)):
        other = neighbour(block, axis, mask)
        block = jnp.concatenate([jnp.where(low, block, other), jnp.where(low, other, block)])
    return block


def gather_ring(block, axis):
    n = lax.axis_size(axis)
    me = lax.axis_index(axis)
    out = jnp.zeros((n, *block.shape), block.dtype)
    for k in range(n):
        part = lax.ppermute(block, axis, [(i, (i + k) % n) for i in range(n)]) if k else block
        out = lax.dynamic_update_index_in_dim(out, part, lax.rem(me - k + n, n), 0)
    return out


def encode(value):
    value = value * 2.0**20
    return (value * jnp.abs(value) * (value * value)).astype(jnp.bfloat16)


def decode(code):
    code = code.astype(jnp.float32)
    inverse = lax.rsqrt(jnp.maximum(jnp.abs(code), 1e-37))
    return (code * inverse) * (inverse * lax.rsqrt(inverse)) * 2.0**-20


def adam_update(clipped, master, first_moment, second_moment):
    new_first = 0.9 * first_moment + 0.1 * clipped
    new_second = 0.95 * second_moment + 0.05 * clipped * clipped
    first_hat = new_first / (1.0 - 0.9**STEP)
    second_hat = new_second / (1.0 - 0.95**STEP)
    update = first_hat / (jnp.sqrt(second_hat) + 1e-08)
    new_master = master - 0.01 * (update + 0.1 * master)
    return (new_master, new_first, new_second)


def clip_factor(squares, width):
    threshold = 4.0 * math.sqrt(D_WIN * width)
    return jnp.minimum(1.0, threshold / (jnp.sqrt(squares) + 1e-06))


def body(grads, master, first_moment, second_moment):
    width = grads.shape[2]
    zh, zl, y, c, x = (lax.axis_size(a) for a in AXES)
    rows = master.shape[0] // x
    me_c, me_x, me_zh = (lax.axis_index(a) for a in ("c", "x", "zh"))

    local = grads[0].reshape(zh, zl, y, c, x, rows, width)
    sent = lax.dynamic_index_in_dim(local, 1 - me_c, 3, keepdims=False)
    kept = lax.dynamic_index_in_dim(local, me_c, 3, keepdims=False)
    pair = kept.astype(jnp.float32) + lax.ppermute(sent, "c", SWAP).astype(jnp.float32)
    coded = encode(pair).transpose(1, 2, 3, 0, 4, 5).reshape(-1, zh * rows, width)
    pieces = lax.all_to_all(coded, PLANE, 0, 0, tiled=True)
    total = sum_of_four(jnp.sum(decode(pieces), axis=0), "zh")

    squares = jnp.sum(to_all(jnp.sum(total * total), OWNERS))
    factor = clip_factor(squares, width)

    mine = factor * lax.dynamic_slice_in_dim(total, me_zh * rows, rows, 0)
    quarter = (lax.dynamic_slice_in_dim(a, me_x * rows, rows, 0) for a in (master, first_moment, second_moment))
    ahead = adam_update(mine, *quarter)[0].astype(jnp.bfloat16)
    gathered = to_all(gather_of_four(ahead, "zh").reshape(-1, width), PLANE)
    owned = gather_ring(mine, "x").reshape(-1, width)
    gathered, owned = lax.optimization_barrier((gathered, owned))
    new_master, new_first, new_second = adam_update(owned, master, first_moment, second_moment)

    other = lax.ppermute(gathered, "c", SWAP)
    weights = jnp.zeros((zh, zl, y, c, x, rows, width), jnp.bfloat16)
    for half, place in ((gathered, me_c), (other, 1 - me_c)):
        half = half.reshape(zl, y, x, zh, rows, width).transpose(3, 0, 1, 2, 4, 5)
        weights = lax.dynamic_update_index_in_dim(weights, half, place, 3)
    return (weights.reshape(-1, width), new_master, new_first, new_second)


def solution(mesh):
    split = Mesh(mesh.devices.reshape(4, 2, 4, 2, mesh.shape["rep"]), AXES)
    dp = AXES[:4]
    placed = (P(AXES, None, None), P(dp, None), P(dp, None), P(dp, None))
    return jax.shard_map(
        body,
        mesh=split,
        in_specs=placed,
        out_specs=(P(), P(dp, None), P(dp, None), P(dp, None)),
        check_vma=False,
    )
```

```python
import math

import jax
import jax.numpy as jnp
from jax import lax
from jax.experimental import pallas as pl
from jax.experimental.pallas import tpu as pltpu
from jax.sharding import Mesh
from jax.sharding import PartitionSpec as P

D_WIN = 4096
STEP = 20
AXES = ("zh", "zl", "y", "c", "x")
PLANE = ("zl", "y", "x")
OWNERS = ("zl", "y", "c", "x")
SWAP = [(0, 1), (1, 0)]


def to_all(block, axes):
    length = lax.axis_size(axes)
    return lax.all_to_all(
        jnp.broadcast_to(block[None], (length, *block.shape)), axes, 0, 0, tiled=True
    )


def neighbour(block, axis, mask):
    return lax.ppermute(block, axis, [(i, i ^ mask) for i in range(4)])


def sum_of_four(block, axis):
    for mask in (1, 3):
        block = block + neighbour(block, axis, mask)
    return block


def doubled(block, axis, mask):
    me = lax.axis_index(axis)
    low = me % 2 == 0 if mask == 1 else me < 2
    other = neighbour(block, axis, mask)
    return jnp.concatenate([jnp.where(low, block, other), jnp.where(low, other, block)])


def around(block, axis):
    n = lax.axis_size(axis)
    ring = {k: lax.ppermute(block, axis, [(i, (i + k) % n) for i in range(n)]) for k in (1, 3, 2)}
    return [block, ring[1], ring[2], ring[3]]


def by_place(parts, axis):
    n = lax.axis_size(axis)
    me = lax.axis_index(axis)
    out = jnp.zeros((n, *parts[0].shape), parts[0].dtype)
    for k, part in enumerate(parts):
        out = lax.dynamic_update_index_in_dim(out, part, lax.rem(me - k + n, n), 0)
    return out


def place(own, xs_ref, ys_ref, own_there, xs_there, ys_there, out, whole, sems):
    zl, y, c, x = (lax.axis_index(a) for a in ("zl", "y", "c", "x"))
    ys = [lax.rem(y - k + 4, 4) for k in range(4)]
    xs = [lax.rem(x - k + 4, 4) for k in range(4)]
    zls = (zl, 1 - zl)
    copies = []
    for zh in range(4):
        half, h = divmod(zh, 2)
        for core, mine, rest in (
            (c, own, (xs_ref, ys_ref)[half]), (1 - c, own_there, (xs_there, ys_there)[half])
        ):
            for j in range(4):
                for k in range(4):
                    at_y, at_x = (ys[k], xs[j]) if half == 0 else (ys[j], xs[k])
                    for l in range(2):
                        piece = rest[j - 1, k, l, h] if j else mine[half, k, l, h]
                        whole[zh, zls[l], at_y, core, at_x] = piece
        copy = pltpu.make_async_copy(whole.at[zh], out.at[zh], sems.at[zh])
        copy.start()
        copies.append(copy)
    for copy in copies:
        copy.wait()


def gather_weights(ahead, mine):
    zh, rows, width = ahead.shape
    high = lax.reduce_precision(mine, 8, 7)
    halves = jnp.stack([high, mine - high]).astype(jnp.bfloat16)
    pair = jnp.stack([ahead, lax.ppermute(ahead, "zl", SWAP)])
    second = pair[:, zh // 2 :].reshape(-1, rows, width)
    second = around(jnp.concatenate([second, halves]), "x")
    owned = by_place([part[4].astype(jnp.float32) + part[5].astype(jnp.float32) for part in second], "x")
    second = jnp.stack([part[:4].reshape(2, 2, rows, width) for part in second])
    first = jnp.stack(around(pair[:, : zh // 2], "y"))
    own = lax.optimization_barrier(jnp.stack([first, second]))
    along_x = jnp.stack(around(own[0], "x")[1:])
    along_y = jnp.stack(around(own[1], "y")[1:])
    here = (own, along_x, along_y)
    there = [lax.ppermute(piece, "c", SWAP) for piece in here]
    shape = (zh, 2, 4, 2, 4, rows, width)
    out = pl.pallas_call(
        place,
        out_shape=jax.ShapeDtypeStruct(shape, ahead.dtype),
        in_specs=[pl.BlockSpec(memory_space=pltpu.VMEM)] * 6,
        out_specs=pl.BlockSpec(memory_space=pl.ANY),
        scratch_shapes=[pltpu.VMEM(shape, ahead.dtype), pltpu.SemaphoreType.DMA((zh,))],
        compiler_params=pltpu.CompilerParams(vmem_limit_bytes=24 * 2**20),
    )(*here, *there)
    return out.reshape(-1, width), owned.reshape(-1, width)


def encode(value):
    value = value * 2.0**20
    return (value * jnp.abs(value) * (value * value)).astype(jnp.bfloat16)


def decode(code):
    code = code.astype(jnp.float32)
    inverse = lax.rsqrt(jnp.maximum(jnp.abs(code), 1e-37))
    return (code * inverse) * (inverse * lax.rsqrt(inverse)) * 2.0**-20


def adam_update(clipped, master, first_moment, second_moment):
    new_first = 0.9 * first_moment + 0.1 * clipped
    new_second = 0.95 * second_moment + 0.05 * clipped * clipped
    first_hat = new_first / (1.0 - 0.9**STEP)
    second_hat = new_second / (1.0 - 0.95**STEP)
    update = first_hat / (jnp.sqrt(second_hat) + 1e-08)
    new_master = master - 0.01 * (update + 0.1 * master)
    return (new_master, new_first, new_second)


def clip_factor(squares, width):
    threshold = 4.0 * math.sqrt(D_WIN * width)
    return jnp.minimum(1.0, threshold / (jnp.sqrt(squares) + 1e-06))


def body(grads, master, first_moment, second_moment):
    width = grads.shape[2]
    zh, zl, y, c, x = (lax.axis_size(a) for a in AXES)
    rows = master.shape[0] // x
    me_c, me_x, me_zh = (lax.axis_index(a) for a in ("c", "x", "zh"))

    states = jnp.stack([
        lax.dynamic_slice_in_dim(a, me_x * rows, rows, 0)
        for a in (master, first_moment, second_moment)
    ])[None]
    states = doubled(states, "zh", 1)

    local = grads[0].reshape(zh, zl, y, c, x, rows, width)
    sent = lax.dynamic_index_in_dim(local, 1 - me_c, 3, keepdims=False)
    kept = lax.dynamic_index_in_dim(local, me_c, 3, keepdims=False)
    pair = kept.astype(jnp.float32) + lax.ppermute(sent, "c", SWAP).astype(jnp.float32)
    coded = encode(pair).transpose(1, 2, 3, 0, 4, 5).reshape(-1, zh * rows, width)
    coded, states = lax.optimization_barrier((coded, states))
    pieces = lax.all_to_all(coded, PLANE, 0, 0, tiled=True)
    total = sum_of_four(jnp.sum(decode(pieces), axis=0), "zh")

    total, states = lax.optimization_barrier((total, states))
    states = doubled(states, "zh", 3)
    squares = jnp.sum(to_all(jnp.sum(total * total), OWNERS))
    factor = clip_factor(squares, width)

    clipped = factor * total
    states = states.transpose(1, 0, 2, 3).reshape(3, -1, width)
    ahead = adam_update(clipped, states[0], states[1], states[2])[0]
    mine = lax.dynamic_slice_in_dim(clipped, me_zh * rows, rows, 0)
    weights, owned = gather_weights(ahead.astype(jnp.bfloat16).reshape(zh, rows, width), mine)
    new_master, new_first, new_second = adam_update(owned, master, first_moment, second_moment)

    return (weights, new_master, new_first, new_second)


def solution(mesh):
    split = Mesh(mesh.devices.reshape(4, 2, 4, 2, mesh.shape["rep"]), AXES)
    dp = AXES[:4]
    placed = (P(AXES, None, None), P(dp, None), P(dp, None), P(dp, None))
    return jax.shard_map(
        body,
        mesh=split,
        in_specs=placed,
        out_specs=(P(), P(dp, None), P(dp, None), P(dp, None)),
        check_vma=False,
    )
```

```python
import math

import jax
import jax.numpy as jnp
from jax import lax
from jax.experimental import pallas as pl
from jax.experimental.pallas import tpu as pltpu
from jax.sharding import Mesh
from jax.sharding import PartitionSpec as P

D_WIN = 4096
STEP = 20
AXES = ("zh", "zl", "y", "c", "x")
PLANE = ("zl", "y", "x")
OWNERS = ("zl", "y", "c", "x")
SWAP = [(0, 1), (1, 0)]


def to_all(block, axes):
    length = lax.axis_size(axes)
    return lax.all_to_all(
        jnp.broadcast_to(block[None], (length, *block.shape)), axes, 0, 0, tiled=True
    )


def neighbour(block, axis, mask):
    return lax.ppermute(block, axis, [(i, i ^ mask) for i in range(4)])


def sum_of_four(block, axis):
    for mask in (1, 3):
        block = block + neighbour(block, axis, mask)
    return block


def interleaved(block, other, axis, mask):
    me = lax.axis_index(axis)
    low = me % 2 == 0 if mask == 1 else me < 2
    return jnp.concatenate([jnp.where(low, block, other), jnp.where(low, other, block)])


def doubled(block, axis, mask):
    return interleaved(block, neighbour(block, axis, mask), axis, mask)


def rows_of_core(local, swapped):
    def kernel(source, out, sem):
        core = lax.axis_index("c")
        copy = pltpu.make_async_copy(source.at[:, 1 - core if swapped else core], out, sem)
        copy.start()
        copy.wait()

    blocks, _, rows, width = local.shape
    return pl.pallas_call(
        kernel,
        out_shape=jax.ShapeDtypeStruct((blocks, rows, width), local.dtype),
        in_specs=[pl.BlockSpec(memory_space=pl.ANY)],
        out_specs=pl.BlockSpec(memory_space=pltpu.VMEM),
        scratch_shapes=[pltpu.SemaphoreType.DMA],
        compiler_params=pltpu.CompilerParams(vmem_limit_bytes=8 * 2**20),
    )(local)


def add_and_encode(ours, theirs, dims):
    zh, zl, y, x, rows, width = dims

    def kernel(ours, theirs, out):
        def step(i, carry):
            for h in range(zh):
                block = h * zl * y + i
                pair = ours[block].astype(jnp.float32) + theirs[block].astype(jnp.float32)
                code = encode(pair)
                for q in range(x):
                    out[i * x + q, h * rows : (h + 1) * rows] = code[q * rows : (q + 1) * rows]
            return carry

        lax.fori_loop(0, zl * y, step, 0)

    return pl.pallas_call(
        kernel,
        out_shape=jax.ShapeDtypeStruct((zl * y * x, zh * rows, width), ours.dtype),
        in_specs=[pl.BlockSpec(memory_space=pltpu.VMEM)] * 2,
        out_specs=pl.BlockSpec(memory_space=pltpu.VMEM),
        compiler_params=pltpu.CompilerParams(vmem_limit_bytes=16 * 2**20),
    )(ours, theirs)


def around(block, axis):
    n = lax.axis_size(axis)
    ring = {k: lax.ppermute(block, axis, [(i, (i + k) % n) for i in range(n)]) for k in (1, 3, 2)}
    return [block, ring[1], ring[2], ring[3]]


def by_place(parts, axis):
    n = lax.axis_size(axis)
    me = lax.axis_index(axis)
    out = jnp.zeros((n, *parts[0].shape), parts[0].dtype)
    for k, part in enumerate(parts):
        out = lax.dynamic_update_index_in_dim(out, part, lax.rem(me - k + n, n), 0)
    return out


def place(own, xs_ref, ys_ref, own_there, xs_there, ys_there, out, whole, sems):
    zl, y, c, x = (lax.axis_index(a) for a in ("zl", "y", "c", "x"))
    ys = [lax.rem(y - k + 4, 4) for k in range(4)]
    xs = [lax.rem(x - k + 4, 4) for k in range(4)]
    zls = (zl, 1 - zl)
    copies = []
    for zh in range(4):
        half, h = divmod(zh, 2)
        for core, mine, rest in (
            (c, own, (xs_ref, ys_ref)[half]), (1 - c, own_there, (xs_there, ys_there)[half])
        ):
            for j in range(4):
                for k in range(4):
                    at_y, at_x = (ys[k], xs[j]) if half == 0 else (ys[j], xs[k])
                    for l in range(2):
                        piece = rest[j - 1, k, l, h] if j else mine[half, k, l, h]
                        whole[zh, zls[l], at_y, core, at_x] = piece
        copy = pltpu.make_async_copy(whole.at[zh], out.at[zh], sems.at[zh])
        copy.start()
        copies.append(copy)
    for copy in copies:
        copy.wait()


def gather_weights(ahead, mine):
    zh, rows, width = ahead.shape
    high = lax.reduce_precision(mine, 8, 7)
    halves = jnp.stack([high, mine - high]).astype(jnp.bfloat16)
    pair = jnp.stack([ahead, lax.ppermute(ahead, "zl", SWAP)])
    second = pair[:, zh // 2 :].reshape(-1, rows, width)
    second = around(jnp.concatenate([second, halves]), "x")
    owned = by_place([part[4].astype(jnp.float32) + part[5].astype(jnp.float32) for part in second], "x")
    second = jnp.stack([part[:4].reshape(2, 2, rows, width) for part in second])
    first = jnp.stack(around(pair[:, : zh // 2], "y"))
    own = lax.optimization_barrier(jnp.stack([first, second]))
    along_x = jnp.stack(around(own[0], "x")[1:])
    along_y = jnp.stack(around(own[1], "y")[1:])
    here = (own, along_x, along_y)
    there = [lax.ppermute(piece, "c", SWAP) for piece in here]
    shape = (zh, 2, 4, 2, 4, rows, width)
    out = pl.pallas_call(
        place,
        out_shape=jax.ShapeDtypeStruct(shape, ahead.dtype),
        in_specs=[pl.BlockSpec(memory_space=pltpu.VMEM)] * 6,
        out_specs=pl.BlockSpec(memory_space=pl.ANY),
        scratch_shapes=[pltpu.VMEM(shape, ahead.dtype), pltpu.SemaphoreType.DMA((zh,))],
        compiler_params=pltpu.CompilerParams(vmem_limit_bytes=24 * 2**20),
    )(*here, *there)
    return out.reshape(-1, width), owned.reshape(-1, width)


def encode(value):
    value = value * 2.0**20
    return (value * jnp.abs(value) * (value * value)).astype(jnp.bfloat16)


def decode(code):
    code = code.astype(jnp.float32)
    inverse = lax.rsqrt(jnp.maximum(jnp.abs(code), 1e-37))
    return (code * inverse) * (inverse * lax.rsqrt(inverse)) * 2.0**-20


def adam_update(clipped, master, first_moment, second_moment):
    new_first = 0.9 * first_moment + 0.1 * clipped
    new_second = 0.95 * second_moment + 0.05 * clipped * clipped
    first_hat = new_first / (1.0 - 0.9**STEP)
    second_hat = new_second / (1.0 - 0.95**STEP)
    update = first_hat / (jnp.sqrt(second_hat) + 1e-08)
    new_master = master - 0.01 * (update + 0.1 * master)
    return (new_master, new_first, new_second)


def clip_factor(squares, width):
    threshold = 4.0 * math.sqrt(D_WIN * width)
    return jnp.minimum(1.0, threshold / (jnp.sqrt(squares) + 1e-06))


def body(grads, master, first_moment, second_moment):
    width = grads.shape[2]
    zh, zl, y, c, x = (lax.axis_size(a) for a in AXES)
    rows = master.shape[0] // x
    me_c, me_x, me_zh = (lax.axis_index(a) for a in ("c", "x", "zh"))

    states = jnp.stack([
        lax.dynamic_slice_in_dim(a, me_x * rows, rows, 0)
        for a in (master, first_moment, second_moment)
    ])[None]
    other_states = neighbour(states, "zh", 1)

    local = grads[0].reshape(-1, c, x * rows, width)
    theirs = rows_of_core(local, True)
    ours = rows_of_core(local, False)
    coded = add_and_encode(ours, lax.ppermute(theirs, "c", SWAP), (zh, zl, y, x, rows, width))
    coded, states, other_states = lax.optimization_barrier((coded, states, other_states))
    states = interleaved(states, other_states, "zh", 1)
    pieces = lax.all_to_all(coded, PLANE, 0, 0, tiled=True)
    total = sum_of_four(jnp.sum(decode(pieces), axis=0), "zh")

    total, states = lax.optimization_barrier((total, states))
    states = doubled(states, "zh", 3)
    squares = jnp.sum(to_all(jnp.sum(total * total), OWNERS))
    factor = clip_factor(squares, width)

    clipped = factor * total
    states = states.transpose(1, 0, 2, 3).reshape(3, -1, width)
    ahead = adam_update(clipped, states[0], states[1], states[2])[0]
    mine = lax.dynamic_slice_in_dim(clipped, me_zh * rows, rows, 0)
    weights, owned = gather_weights(ahead.astype(jnp.bfloat16).reshape(zh, rows, width), mine)
    new_master, new_first, new_second = adam_update(owned, master, first_moment, second_moment)

    return (weights, new_master, new_first, new_second)


def solution(mesh):
    split = Mesh(mesh.devices.reshape(4, 2, 4, 2, mesh.shape["rep"]), AXES)
    dp = AXES[:4]
    placed = (P(AXES, None, None), P(dp, None), P(dp, None), P(dp, None))
    return jax.shard_map(
        body,
        mesh=split,
        in_specs=placed,
        out_specs=(P(), P(dp, None), P(dp, None), P(dp, None)),
        check_vma=False,
    )
```

```python
import math

import jax
import jax.numpy as jnp
from jax import lax
from jax.experimental import pallas as pl
from jax.experimental.pallas import tpu as pltpu
from jax.sharding import Mesh
from jax.sharding import PartitionSpec as P

D_WIN = 4096
STEP = 20
AXES = ("zh", "zl", "y", "c", "x")
PLANE = ("zl", "y", "x")
OWNERS = ("zl", "y", "c", "x")
SWAP = [(0, 1), (1, 0)]


def to_all(block, axes):
    length = lax.axis_size(axes)
    return lax.all_to_all(
        jnp.broadcast_to(block[None], (length, *block.shape)), axes, 0, 0, tiled=True
    )


def neighbour(block, axis, mask):
    return lax.ppermute(block, axis, [(i, i ^ mask) for i in range(4)])


def sum_of_four(block, axis):
    for mask in (1, 3):
        block = block + neighbour(block, axis, mask)
    return block


def interleaved(block, other, axis, mask):
    me = lax.axis_index(axis)
    low = me % 2 == 0 if mask == 1 else me < 2
    return jnp.concatenate([jnp.where(low, block, other), jnp.where(low, other, block)])


def rows_of_core(local, swapped):
    def kernel(source, out, sem):
        core = lax.axis_index("c")
        copy = pltpu.make_async_copy(source.at[:, 1 - core if swapped else core], out, sem)
        copy.start()
        copy.wait()

    blocks, _, rows, width = local.shape
    return pl.pallas_call(
        kernel,
        out_shape=jax.ShapeDtypeStruct((blocks, rows, width), local.dtype),
        in_specs=[pl.BlockSpec(memory_space=pl.ANY)],
        out_specs=pl.BlockSpec(memory_space=pltpu.VMEM),
        scratch_shapes=[pltpu.SemaphoreType.DMA],
        compiler_params=pltpu.CompilerParams(vmem_limit_bytes=8 * 2**20),
    )(local)


def add_and_encode(ours, theirs, dims):
    zh, zl, y, x, rows, width = dims

    def kernel(ours, theirs, out):
        def step(i, carry):
            for h in range(zh):
                block = h * zl * y + i
                pair = ours[block].astype(jnp.float32) + theirs[block].astype(jnp.float32)
                code = encode(pair)
                for q in range(x):
                    out[i * x + q, h * rows : (h + 1) * rows] = code[q * rows : (q + 1) * rows]
            return carry

        lax.fori_loop(0, zl * y, step, 0)

    return pl.pallas_call(
        kernel,
        out_shape=jax.ShapeDtypeStruct((zl * y * x, zh * rows, width), ours.dtype),
        in_specs=[pl.BlockSpec(memory_space=pltpu.VMEM)] * 2,
        out_specs=pl.BlockSpec(memory_space=pltpu.VMEM),
        compiler_params=pltpu.CompilerParams(vmem_limit_bytes=16 * 2**20),
    )(ours, theirs)


def around(block, axis):
    n = lax.axis_size(axis)
    ring = {k: lax.ppermute(block, axis, [(i, (i + k) % n) for i in range(n)]) for k in (1, 3, 2)}
    return [block, ring[1], ring[2], ring[3]]


def by_place(parts, axis):
    n = lax.axis_size(axis)
    me = lax.axis_index(axis)
    out = jnp.zeros((n, *parts[0].shape), parts[0].dtype)
    for k, part in enumerate(parts):
        out = lax.dynamic_update_index_in_dim(out, part, lax.rem(me - k + n, n), 0)
    return out


def place(own, xs_ref, ys_ref, own_there, xs_there, ys_there, out, whole, sems):
    zl, y, c, x = (lax.axis_index(a) for a in ("zl", "y", "c", "x"))
    ys = [lax.rem(y - k + 4, 4) for k in range(4)]
    xs = [lax.rem(x - k + 4, 4) for k in range(4)]
    zls = (zl, 1 - zl)
    copies = []
    for zh in range(4):
        half, h = divmod(zh, 2)
        for core, mine, rest in (
            (c, own, (xs_ref, ys_ref)[half]), (1 - c, own_there, (xs_there, ys_there)[half])
        ):
            for j in range(4):
                for k in range(4):
                    at_y, at_x = (ys[k], xs[j]) if half == 0 else (ys[j], xs[k])
                    for l in range(2):
                        piece = rest[j - 1, k, l, h] if j else mine[half, k, l, h]
                        whole[zh, zls[l], at_y, core, at_x] = piece
        copy = pltpu.make_async_copy(whole.at[zh], out.at[zh], sems.at[zh])
        copy.start()
        copies.append(copy)
    for copy in copies:
        copy.wait()


def gather_weights(ahead, mine):
    zh, rows, width = ahead.shape
    high = lax.reduce_precision(mine, 8, 7)
    halves = jnp.stack([high, mine - high]).astype(jnp.bfloat16)
    pair = jnp.stack([ahead, lax.ppermute(ahead, "zl", SWAP)])
    second = pair[:, zh // 2 :].reshape(-1, rows, width)
    second = around(jnp.concatenate([second, halves]), "x")
    owned = by_place([part[4].astype(jnp.float32) + part[5].astype(jnp.float32) for part in second], "x")
    second = jnp.stack([part[:4].reshape(2, 2, rows, width) for part in second])
    first = jnp.stack(around(pair[:, : zh // 2], "y"))
    own = lax.optimization_barrier(jnp.stack([first, second]))
    along_x = jnp.stack(around(own[0], "x")[1:])
    along_y = jnp.stack(around(own[1], "y")[1:])
    here = (own, along_x, along_y)
    there = [lax.ppermute(piece, "c", SWAP) for piece in here]
    shape = (zh, 2, 4, 2, 4, rows, width)
    out = pl.pallas_call(
        place,
        out_shape=jax.ShapeDtypeStruct(shape, ahead.dtype),
        in_specs=[pl.BlockSpec(memory_space=pltpu.VMEM)] * 6,
        out_specs=pl.BlockSpec(memory_space=pl.ANY),
        scratch_shapes=[pltpu.VMEM(shape, ahead.dtype), pltpu.SemaphoreType.DMA((zh,))],
        compiler_params=pltpu.CompilerParams(vmem_limit_bytes=24 * 2**20),
    )(*here, *there)
    return out.reshape(-1, width), owned.reshape(-1, width)


def encode(value):
    value = value * 2.0**20
    return (value * jnp.abs(value) * (value * value)).astype(jnp.bfloat16)


def decode(code):
    code = code.astype(jnp.float32)
    inverse = lax.rsqrt(jnp.maximum(jnp.abs(code), 1e-37))
    return (code * inverse) * (inverse * lax.rsqrt(inverse)) * 2.0**-20


def adam_update(clipped, master, first_moment, second_moment):
    new_first = 0.9 * first_moment + 0.1 * clipped
    new_second = 0.95 * second_moment + 0.05 * clipped * clipped
    first_hat = new_first / (1.0 - 0.9**STEP)
    second_hat = new_second / (1.0 - 0.95**STEP)
    update = first_hat / (jnp.sqrt(second_hat) + 1e-08)
    new_master = master - 0.01 * (update + 0.1 * master)
    return (new_master, new_first, new_second)


def clip_factor(squares, width):
    threshold = 4.0 * math.sqrt(D_WIN * width)
    return jnp.minimum(1.0, threshold / (jnp.sqrt(squares) + 1e-06))


def body(grads, master, first_moment, second_moment):
    width = grads.shape[2]
    zh, zl, y, c, x = (lax.axis_size(a) for a in AXES)
    rows = master.shape[0] // x
    me_c, me_x, me_zh = (lax.axis_index(a) for a in ("c", "x", "zh"))

    states = jnp.stack([
        lax.dynamic_slice_in_dim(a, me_x * rows, rows, 0)
        for a in (master, first_moment, second_moment)
    ])[None]
    other_states = neighbour(states, "zh", 1)

    local = grads[0].reshape(-1, c, x * rows, width)
    theirs = rows_of_core(local, True)
    ours = rows_of_core(local, False)
    coded = add_and_encode(ours, lax.ppermute(theirs, "c", SWAP), (zh, zl, y, x, rows, width))
    coded, states, other_states = lax.optimization_barrier((coded, states, other_states))
    coded, states = lax.optimization_barrier((coded, interleaved(states, other_states, "zh", 1)))
    pieces = lax.all_to_all(coded, PLANE, 0, 0, tiled=True)
    partial, states = lax.optimization_barrier((jnp.sum(decode(pieces), axis=0), states))
    other_states = neighbour(states, "zh", 3)
    total = sum_of_four(partial, "zh")

    total, states, other_states = lax.optimization_barrier((total, states, other_states))
    states = interleaved(states, other_states, "zh", 3)
    squares = jnp.sum(to_all(jnp.sum(total * total), OWNERS))
    factor = clip_factor(squares, width)

    clipped = factor * total
    states = states.transpose(1, 0, 2, 3).reshape(3, -1, width)
    ahead = adam_update(clipped, states[0], states[1], states[2])[0]
    mine = lax.dynamic_slice_in_dim(clipped, me_zh * rows, rows, 0)
    weights, owned = gather_weights(ahead.astype(jnp.bfloat16).reshape(zh, rows, width), mine)
    new_master, new_first, new_second = adam_update(owned, master, first_moment, second_moment)

    return (weights, new_master, new_first, new_second)


def solution(mesh):
    split = Mesh(mesh.devices.reshape(4, 2, 4, 2, mesh.shape["rep"]), AXES)
    dp = AXES[:4]
    placed = (P(AXES, None, None), P(dp, None), P(dp, None), P(dp, None))
    return jax.shard_map(
        body,
        mesh=split,
        in_specs=placed,
        out_specs=(P(), P(dp, None), P(dp, None), P(dp, None)),
        check_vma=False,
    )
```

```python
import math

import jax
import jax.numpy as jnp
from jax import lax
from jax.experimental import pallas as pl
from jax.experimental.pallas import tpu as pltpu
from jax.sharding import Mesh
from jax.sharding import PartitionSpec as P

D_WIN = 4096
STEP = 20
AXES = ("zh", "zl", "y", "c", "x")
PLANE = ("zl", "y", "x")
OWNERS = ("zl", "y", "c", "x")
SWAP = [(0, 1), (1, 0)]


def to_all(block, axes):
    length = lax.axis_size(axes)
    return lax.all_to_all(
        jnp.broadcast_to(block[None], (length, *block.shape)), axes, 0, 0, tiled=True
    )


def neighbour(block, axis, mask):
    return lax.ppermute(block, axis, [(i, i ^ mask) for i in range(4)])


def sum_of_four(block, axis):
    for mask in (1, 3):
        block = block + neighbour(block, axis, mask)
    return block


def interleaved(block, other, axis, mask):
    me = lax.axis_index(axis)
    low = me % 2 == 0 if mask == 1 else me < 2
    return jnp.concatenate([jnp.where(low, block, other), jnp.where(low, other, block)])


def rows_of_core(local):
    def kernel(source, out, sem):
        core = lax.axis_index("c")
        copy = pltpu.make_async_copy(source.at[:, core], out, sem)
        copy.start()
        copy.wait()

    blocks, _, rows, width = local.shape
    return pl.pallas_call(
        kernel,
        out_shape=jax.ShapeDtypeStruct((blocks, rows, width), local.dtype),
        in_specs=[pl.BlockSpec(memory_space=pl.ANY)],
        out_specs=pl.BlockSpec(memory_space=pltpu.VMEM),
        scratch_shapes=[pltpu.SemaphoreType.DMA],
        compiler_params=pltpu.CompilerParams(vmem_limit_bytes=8 * 2**20),
    )(local)


def add_and_encode(ours, theirs, dims):
    zh, zl, y, x, rows, width = dims

    def kernel(ours, theirs, out):
        def step(i, carry):
            for h in range(zh):
                block = h * zl * y + i
                pair = ours[block].astype(jnp.float32) + theirs[block].astype(jnp.float32)
                code = encode(pair)
                for q in range(x):
                    out[i * x + q, h * rows : (h + 1) * rows] = code[q * rows : (q + 1) * rows]
            return carry

        lax.fori_loop(0, zl * y, step, 0)

    return pl.pallas_call(
        kernel,
        out_shape=jax.ShapeDtypeStruct((zl * y * x, zh * rows, width), ours.dtype),
        in_specs=[pl.BlockSpec(memory_space=pltpu.VMEM)] * 2,
        out_specs=pl.BlockSpec(memory_space=pltpu.VMEM),
        compiler_params=pltpu.CompilerParams(vmem_limit_bytes=16 * 2**20),
    )(ours, theirs)


def around(block, axis):
    n = lax.axis_size(axis)
    ring = {k: lax.ppermute(block, axis, [(i, (i + k) % n) for i in range(n)]) for k in (1, 3, 2)}
    return [block, ring[1], ring[2], ring[3]]


def by_place(parts, axis):
    n = lax.axis_size(axis)
    me = lax.axis_index(axis)
    out = jnp.zeros((n, *parts[0].shape), parts[0].dtype)
    for k, part in enumerate(parts):
        out = lax.dynamic_update_index_in_dim(out, part, lax.rem(me - k + n, n), 0)
    return out


def place(own, xs_ref, ys_ref, own_there, xs_there, ys_there, out, whole, sems):
    zl, y, c, x = (lax.axis_index(a) for a in ("zl", "y", "c", "x"))
    ys = [lax.rem(y - k + 4, 4) for k in range(4)]
    xs = [lax.rem(x - k + 4, 4) for k in range(4)]
    zls = (zl, 1 - zl)
    copies = []
    for zh in range(4):
        half, h = divmod(zh, 2)
        for core, mine, rest in (
            (c, own, (xs_ref, ys_ref)[half]), (1 - c, own_there, (xs_there, ys_there)[half])
        ):
            for j in range(4):
                for k in range(4):
                    at_y, at_x = (ys[k], xs[j]) if half == 0 else (ys[j], xs[k])
                    for l in range(2):
                        piece = rest[j - 1, k, l, h] if j else mine[half, k, l, h]
                        whole[zh, zls[l], at_y, core, at_x] = piece
        copy = pltpu.make_async_copy(whole.at[zh], out.at[zh], sems.at[zh])
        copy.start()
        copies.append(copy)
    for copy in copies:
        copy.wait()


def gather_weights(ahead, mine):
    zh, rows, width = ahead.shape
    high = lax.reduce_precision(mine, 8, 7)
    halves = jnp.stack([high, mine - high]).astype(jnp.bfloat16)
    pair = jnp.stack([ahead, lax.ppermute(ahead, "zl", SWAP)])
    second = pair[:, zh // 2 :].reshape(-1, rows, width)
    second = around(jnp.concatenate([second, halves]), "x")
    owned = by_place([part[4].astype(jnp.float32) + part[5].astype(jnp.float32) for part in second], "x")
    second = jnp.stack([part[:4].reshape(2, 2, rows, width) for part in second])
    first = jnp.stack(around(pair[:, : zh // 2], "y"))
    own = lax.optimization_barrier(jnp.stack([first, second]))
    along_x = jnp.stack(around(own[0], "x")[1:])
    along_y = jnp.stack(around(own[1], "y")[1:])
    here = (own, along_x, along_y)
    there = [lax.ppermute(piece, "c", SWAP) for piece in here]
    shape = (zh, 2, 4, 2, 4, rows, width)
    out = pl.pallas_call(
        place,
        out_shape=jax.ShapeDtypeStruct(shape, ahead.dtype),
        in_specs=[pl.BlockSpec(memory_space=pltpu.VMEM)] * 6,
        out_specs=pl.BlockSpec(memory_space=pl.ANY),
        scratch_shapes=[pltpu.VMEM(shape, ahead.dtype), pltpu.SemaphoreType.DMA((zh,))],
        compiler_params=pltpu.CompilerParams(vmem_limit_bytes=24 * 2**20),
    )(*here, *there)
    return out.reshape(-1, width), owned.reshape(-1, width)


def encode(value):
    value = value * 2.0**20
    return (value * jnp.abs(value) * (value * value)).astype(jnp.bfloat16)


def decode(code):
    code = code.astype(jnp.float32)
    inverse = lax.rsqrt(jnp.maximum(jnp.abs(code), 1e-37))
    return (code * inverse) * (inverse * lax.rsqrt(inverse)) * 2.0**-20


def adam_update(clipped, master, first_moment, second_moment):
    new_first = 0.9 * first_moment + 0.1 * clipped
    new_second = 0.95 * second_moment + 0.05 * clipped * clipped
    first_hat = new_first / (1.0 - 0.9**STEP)
    second_hat = new_second / (1.0 - 0.95**STEP)
    update = first_hat / (jnp.sqrt(second_hat) + 1e-08)
    new_master = master - 0.01 * (update + 0.1 * master)
    return (new_master, new_first, new_second)


def clip_factor(squares, width):
    threshold = 4.0 * math.sqrt(D_WIN * width)
    return jnp.minimum(1.0, threshold / (jnp.sqrt(squares) + 1e-06))


def body(grads, master, first_moment, second_moment):
    width = grads.shape[2]
    zh, zl, y, c, x = (lax.axis_size(a) for a in AXES)
    rows = master.shape[0] // x
    me_c, me_x, me_zh = (lax.axis_index(a) for a in ("c", "x", "zh"))

    states = jnp.stack([
        lax.dynamic_slice_in_dim(a, me_x * rows, rows, 0)
        for a in (master, first_moment, second_moment)
    ])[None]
    other_states = neighbour(states, "zh", 1)

    local = grads[0].reshape(-1, c, x * rows, width)
    theirs = lax.dynamic_index_in_dim(local, 1 - lax.axis_index("c"), 1, keepdims=False)
    ours = rows_of_core(local)
    coded = add_and_encode(ours, lax.ppermute(theirs, "c", SWAP), (zh, zl, y, x, rows, width))
    coded, states, other_states = lax.optimization_barrier((coded, states, other_states))
    coded, states = lax.optimization_barrier((coded, interleaved(states, other_states, "zh", 1)))
    pieces = lax.all_to_all(coded, PLANE, 0, 0, tiled=True)
    partial, states = lax.optimization_barrier((jnp.sum(decode(pieces), axis=0), states))
    other_states = neighbour(states, "zh", 3)
    total = sum_of_four(partial, "zh")

    total, states, other_states = lax.optimization_barrier((total, states, other_states))
    states = interleaved(states, other_states, "zh", 3)
    squares = jnp.sum(to_all(jnp.sum(total * total), OWNERS))
    factor = clip_factor(squares, width)

    clipped = factor * total
    states = states.transpose(1, 0, 2, 3).reshape(3, -1, width)
    ahead = adam_update(clipped, states[0], states[1], states[2])[0]
    mine = lax.dynamic_slice_in_dim(clipped, me_zh * rows, rows, 0)
    weights, owned = gather_weights(ahead.astype(jnp.bfloat16).reshape(zh, rows, width), mine)
    new_master, new_first, new_second = adam_update(owned, master, first_moment, second_moment)

    return (weights, new_master, new_first, new_second)


def solution(mesh):
    split = Mesh(mesh.devices.reshape(4, 2, 4, 2, mesh.shape["rep"]), AXES)
    dp = AXES[:4]
    placed = (P(AXES, None, None), P(dp, None), P(dp, None), P(dp, None))
    return jax.shard_map(
        body,
        mesh=split,
        in_specs=placed,
        out_specs=(P(), P(dp, None), P(dp, None), P(dp, None)),
        check_vma=False,
    )
```
